512 devices in a mesh: dp: 64 (over z_hi, x, y), tensor: 8 (over z_lo, core).
Axes of the slice: x: 4, y: 4, z: 16 (z_hi: 4, z_lo: 4; z = z_hi * 4 + z_lo), core: 2. Of those that a mesh axis runs over, the one named last changes fastest.
Arguments:
- activations: bfloat16 [32768, 8192], P('dp', 'tensor'), may hold values from -6 to 6
- projection_basis: bfloat16 [8192, 512], P('tensor'), may hold values from -0.0625 to 0.0625
- cotangent: bfloat16 [64, 8, 28, 32768], P(None, 'tensor', None, 'dp'), may hold values from -0.09375 to 0.09375
- first_moment: float32 [64, 8, 28, 512], P('dp', 'tensor'), may hold values from -3 to 3
- second_moment: float32 [64, 8, 28, 512], P('dp', 'tensor'), may hold values from 0.05 to 2
Outputs:
- new_first: float32 [64, 8, 28, 512], P('dp', 'tensor')
- new_second: float32 [64, 8, 28, 512], P('dp', 'tensor')
- weight_update: bfloat16 [8192, 64, 224], P('tensor', 'dp')
The draws below stay inside these ranges and needn't reach their ends.
All inputs are finite; a program needn't handle non-finite values.
Results may differ from the reference program's by a relative error of at most 0.005.
Values may be sent and summed in bfloat16 or wider, within the bound.
A program may use at most 64 MiB of HBM per device.

```python
import math
import jax
import jax.numpy as jnp
from jax import lax

D = 8192
R = 512
COLS = 28
STEP = 100
TOKENS = 32768
BLOCKS = 64
SUBS = 8


def raised(drawn, rng, source, target, blocks, factor):
    def block_of(axis_at):
        return (jnp.arange(drawn.shape[axis_at]) // (drawn.shape[axis_at] // blocks)).reshape((-1,) + (1,) * (drawn.ndim - 1 - axis_at))

    one_side = jax.random.permutation(rng, blocks)[block_of(target)]
    other_side = (block_of(target) + blocks // 2) % blocks
    return jnp.where((block_of(source) == one_side) | (block_of(source) == other_side), factor * drawn, drawn)


def block_levels(stream_key, dims, pieces, least, top_value):
    gain = 1.0
    for dim, parts in pieces:
        draws = jax.random.uniform(jax.random.fold_in(jax.random.fold_in(stream_key, 6), dim), (parts,), jnp.float32, least / len(pieces), top_value / len(pieces))
        gain = gain * jnp.repeat(jnp.exp(draws), dims[dim] // parts).reshape((-1,) + (1,) * (len(dims) - 1 - dim))
    return gain


def normal_values(stream_key, dims, deviation, limit, pieces=(), held_as=jnp.bfloat16):
    gain = block_levels(stream_key, dims, pieces, -0.22, 0.18) if pieces else 1.0
    drawn = jax.random.normal(stream_key, dims, jnp.float32) * deviation * gain
    return jnp.minimum(jnp.maximum(drawn, -limit), limit).astype(held_as)


def gaussian_with(rng, extent, spread, reach, shards, heavy, dtype=jnp.bfloat16):
    array = spread * jax.random.normal(rng, extent, jnp.float32)
    if shards:
        array = array * block_levels(rng, extent, shards, -0.22, 0.18)
    return jnp.clip(raised(array, jax.random.fold_in(rng, 3), *heavy), -reach, reach).astype(dtype)


def setup_inputs(seed: int = 0) -> dict:
    splits = jax.random.split(jax.random.key(seed), 6)
    activations = normal_values(splits[0], (TOKENS, D), 1.0, 6.0, ((0, 64), (1, 8)))
    projection_basis = normal_values(splits[1], (D, R), D ** -0.5, 0.0625, ((0, 8),))
    cotangent = gaussian_with(splits[2], (BLOCKS, SUBS, COLS, TOKENS), TOKENS ** -0.5, 0.09375, ((1, 8), (3, 64)), (3, 0, 64, 4.0))
    first_moment = normal_values(splits[3], (BLOCKS, SUBS, COLS, R), 0.5, 3.0, ((0, 64), (1, 8)), jnp.float32)
    second_moment = jnp.clip(jnp.exp(math.log(2.0) - 3.6888794 * jax.random.uniform(splits[4], (BLOCKS, SUBS, COLS, R), jnp.float32) ** block_levels(splits[4], (BLOCKS, SUBS, COLS, R), ((0, 64), (1, 8)), -0.2, 0.2)), 0.05, 2.0)
    return dict(activations=activations, projection_basis=projection_basis, cotangent=cotangent, first_moment=first_moment, second_moment=second_moment)


def reference(activations, projection_basis, cotangent, first_moment, second_moment):
    projected = jnp.dot(activations, projection_basis, preferred_element_type=jnp.float32).astype(jnp.bfloat16)
    cotangent_rows = cotangent.reshape(BLOCKS * SUBS * COLS, TOKENS)
    low_rank_grad = jnp.dot(cotangent_rows, projected, preferred_element_type=jnp.float32)
    low_rank_grad = low_rank_grad.reshape(BLOCKS, SUBS, COLS, R)
    new_first = 0.9 * first_moment + 0.1 * low_rank_grad
    new_second = 0.999 * second_moment + 0.001 * low_rank_grad * low_rank_grad
    first_scale = 1.0 - 0.9 ** STEP
    second_scale = 1.0 - 0.999 ** STEP
    direction = new_first / first_scale / (jnp.sqrt(new_second / second_scale) + 1e-08)
    direction = direction.astype(jnp.bfloat16).reshape(BLOCKS * SUBS * COLS, R)
    update_full = lax.dot_general(projection_basis, direction, (((1,), (1,)), ((), ())), preferred_element_type=jnp.float32)
    weight_update = update_full.astype(jnp.bfloat16).reshape(D, BLOCKS, SUBS * COLS)
    return (new_first, new_second, weight_update)
```

```python
import functools

import jax
import jax.numpy as jnp
from jax import lax
from jax.experimental import pallas as pl
from jax.experimental.pallas import tpu as pltpu
from jax.sharding import PartitionSpec as P

STEP = 100
CH = 4
KC = 128
SLOTS = 21
MESH = pl.DeviceIdType.MESH
F32, BF16 = jnp.float32, jnp.bfloat16

X0, E, M, T, TC, XY1, XY2, ZH, AG, AGC = 0, 1, 2, 3, 4, 5, 8, 11, 14, 17


def kernel(
    act_hbm, basis_hbm, cot_hbm, m1_hbm, m2_hbm,
    nf_ref, ns_ref, wu_ref,
    act, basis, cot, cotf, cperm, m1, m2, nfs, nss,
    x0s, x0r, acc, sb, er, mb, mr, proj,
    p2, r1, g, r2, hs, zs, r3, dirs, wide, lhs,
    in_sem, send_sem, recv_sem,
):
    dp, tensor = lax.axis_index("dp"), lax.axis_index("tensor")
    zh, x, y = dp // 16, (dp // 4) % 4, dp % 4
    zl, c = tensor // 2, tensor % 2
    mid = jnp.logical_or(zl == 1, zl == 2)
    end = jnp.logical_not(mid)

    def at(zh=zh, x=x, y=y, zl=zl, c=c):
        return (zh * 16 + x * 4 + y, zl * 2 + c)

    def turn(v, i):
        return (v + i) % 4

    other_core = at(c=1 - c)
    pair = at(zl=zl + 1 - 2 * (zl % 2))
    middle = at(zl=3 - zl)
    xs = [at(x=turn(x, i)) for i in (1, 2, 3)]
    ys = [at(y=turn(y, i)) for i in (1, 2, 3)]
    zhs = [at(zh=turn(zh, i)) for i in (1, 2, 3)]
    zls = [at(zl=turn(zl, i)) for i in (1, 2, 3)]

    barrier = pltpu.get_barrier_semaphore()
    for device in [other_core] + zls + xs + ys + zhs:
        pl.semaphore_signal(barrier, inc=1, device_id=device, device_id_type=MESH)

    loads = [
        pltpu.make_async_copy(act_hbm, act, in_sem.at[0]),
        pltpu.make_async_copy(basis_hbm, basis, in_sem.at[1]),
        pltpu.make_async_copy(cot_hbm, cot, in_sem.at[2]),
        pltpu.make_async_copy(m1_hbm, m1.at[pl.ds(0, 112)], in_sem.at[3]),
        pltpu.make_async_copy(m2_hbm, m2.at[pl.ds(0, 112)], in_sem.at[4]),
    ]
    for load in loads:
        load.start()

    def copy(k, slot, src, dst, device):
        i = k * SLOTS + slot
        return pltpu.make_async_remote_copy(
            src, dst, send_sem.at[i], recv_sem.at[i], device_id=device, device_id_type=MESH
        )

    mine = pl.ds(pl.multiple_of(c * 256, 256), 256)
    theirs = pl.ds(pl.multiple_of((1 - c) * 256, 256), 256)

    def cp_x0(k):
        return copy(k, X0, x0s.at[k], x0r.at[k], other_core)

    def cp_e(k):
        return copy(k, E, sb.at[k], er.at[k], pair)

    def cp_m(k):
        return copy(k, M, mb.at[k], mr.at[k], middle)

    def cp_t(k):
        return copy(k, T, proj.at[k, mine], proj.at[k, mine], pair)

    def cp_tc(k):
        return copy(k, TC, proj.at[k, mine], proj.at[k, mine], other_core)

    def tc_arrival(k):
        return copy(k, TC, proj.at[k, theirs], proj.at[k, theirs], other_core)

    def cp_1(k, i):
        if k % 2 == 0:
            return copy(k, XY1 + i, p2.at[k, turn(x, i + 1)], r1.at[k, i], xs[i])
        return copy(k, XY1 + i, p2.at[k, :, turn(y, i + 1)], r1.at[k, i], ys[i])

    def cp_2(k, i):
        if k % 2 == 0:
            return copy(k, XY2 + i, g.at[k, turn(y, i + 1)], r2.at[k, i], ys[i])
        return copy(k, XY2 + i, g.at[k, turn(x, i + 1)], r2.at[k, i], xs[i])

    def cp_z(k, i):
        return copy(k, ZH + i, zs.at[k, turn(zh, i + 1)], r3.at[k, i], zhs[i])

    def cp_ag(k, i):
        return copy(k, AG + i, dirs.at[k, tensor], dirs.at[k, tensor], zls[i])

    def ag_arrival(k, i):
        slot = dirs.at[k, turn(zl, 3 - i) * 2 + c]
        return copy(k, AG + i, slot, slot, zls[i])

    def cp_agc(k, i):
        slot = dirs.at[k, turn(zl, 4 - i) * 2 + c]
        return copy(k, AGC + i, slot, slot, other_core)

    def agc_arrival(k, i):
        slot = dirs.at[k, turn(zl, 4 - i) * 2 + 1 - c]
        return copy(k, AGC + i, slot, slot, other_core)

    for buf in (hs,):
        for k in range(CH):
            buf[k, pl.ds(112, 16)] = jnp.zeros((16, KC), F32)
    m1[pl.ds(112, 16)] = jnp.zeros((16, KC), F32)
    m2[pl.ds(112, 16)] = jnp.zeros((16, KC), F32)
    loads[0].wait()
    loads[1].wait()
    out = jnp.dot(act[theirs, :], basis[...], preferred_element_type=F32)
    for k in range(CH):
        x0s[k] = out[:, k * KC : (k + 1) * KC].astype(BF16)
    out = jnp.dot(act[mine, :], basis[...], preferred_element_type=F32)
    for k in range(CH):
        acc[k] = out[:, k * KC : (k + 1) * KC]
    loads[2].wait()
    for n in range(4):
        cotf[n] = cot[:, n * 128 : (n + 1) * 128].astype(F32)
    for n in range(4):
        for b in range(16):
            cperm[pl.ds(b * 112, 112), n * 128 : (n + 1) * 128] = cotf[n, pl.ds(b, 112, stride=16), :].astype(BF16)
    pl.semaphore_wait(barrier, 13)

    def s0(k):
        cp_x0(k).start()

    def s1(k):
        cp_x0(k).wait_recv()
        total = acc[k] + x0r[k].astype(F32)
        acc[k] = total

        @pl.when(end)
        def _():
            sb[k] = total.astype(BF16)
            cp_e(k).start()

    def s2(k):
        @pl.when(mid)
        def _():
            cp_e(k).wait_recv()
            total = acc[k] + er[k].astype(F32)
            acc[k] = total
            mb[k] = total.astype(BF16)
            cp_m(k).start()

    def s3(k):
        @pl.when(mid)
        def _():
            cp_m(k).wait_recv()
            proj[k, mine] = (acc[k] + mr[k].astype(F32)).astype(BF16)
            cp_t(k).start()

        @pl.when(end)
        def _():
            cp_t(k).wait_recv()

        cp_tc(k).start()

    def s4(k):
        tc_arrival(k).wait_recv()
        out = jnp.dot(cperm[...], proj[k], preferred_element_type=F32)
        p2[k] = out.astype(BF16).reshape(4, 4, 112, KC)
        for i in range(3):
            cp_1(k, i).start()

    def s5(k):
        own = p2[k, x] if k % 2 == 0 else p2[k, :, y]
        total = own.astype(F32)
        for i in range(3):
            cp_1(k, i).wait_recv()
            total = total + r1[k, i].astype(F32)
        g[k] = total.astype(BF16)
        for i in range(3):
            cp_2(k, i).start()

    def s6(k):
        own = g[k, y] if k % 2 == 0 else g[k, x]
        total = own.astype(F32)
        for i in range(3):
            cp_2(k, i).wait_recv()
            total = total + r2[k, i].astype(F32)
        hs[k, pl.ds(0, 112)] = total
        for z in range(4):
            zs[k, z] = hs[k, pl.ds(z, 32, stride=4), :].astype(BF16)
        for i in range(3):
            cp_z(k, i).start()

    def s7(k):
        grad = zs[k, zh].astype(F32)
        for i in range(3):
            cp_z(k, i).wait_recv()
            grad = grad + r3[k, i].astype(F32)
        rows = pl.ds(k, 32, stride=4)
        new_first = 0.9 * m1[rows, :] + 0.1 * grad
        new_second = 0.999 * m2[rows, :] + 0.001 * grad * grad
        nfs[rows, :] = new_first
        nss[rows, :] = new_second
        direction = new_first / (1.0 - 0.9**STEP) / (jnp.sqrt(new_second / (1.0 - 0.999**STEP)) + 1e-08)
        dirs[k, tensor] = direction.astype(BF16)
        for i in range(3):
            cp_ag(k, i).start()
        cp_agc(k, 0).start()

    def s8(k):
        for i in range(3):
            ag_arrival(k, i).wait_recv()
            cp_agc(k, i + 1).start()

    def s9(k):
        for i in range(4):
            agc_arrival(k, i).wait_recv()
        for t in range(8):
            wide[k, pl.ds(t * 28, 32)] = dirs[k, t].astype(F32)
        lhs[:, k * KC : (k + 1) * KC] = wide[k, pl.ds(0, 224)].astype(BF16)

    for stage in (s0, s1, s2, s3, s4, s5, s6):
        for k in range(CH):
            stage(k)
    loads[3].wait()
    loads[4].wait()
    for stage in (s7, s8, s9):
        for k in range(CH):
            stage(k)
    nf_ref[...] = nfs[pl.ds(0, 112)]
    ns_ref[...] = nss[pl.ds(0, 112)]
    wu_ref[...] = lax.dot_general(
        lhs[...], basis[...], (((1,), (1,)), ((), ())), preferred_element_type=F32
    ).astype(BF16)

    for k in range(CH):
        cp_x0(k).wait_send()
        cp_tc(k).wait_send()
        for i in range(3):
            cp_1(k, i).wait_send()
            cp_2(k, i).wait_send()
            cp_z(k, i).wait_send()
            cp_ag(k, i).wait_send()
        for i in range(4):
            cp_agc(k, i).wait_send()

    @pl.when(end)
    def _():
        for k in range(CH):
            cp_e(k).wait_send()

    @pl.when(mid)
    def _():
        for k in range(CH):
            cp_m(k).wait_send()
            cp_t(k).wait_send()


def per_device(activations, projection_basis, cotangent, first_moment, second_moment):
    cot = jnp.transpose(cotangent, (1, 2, 0, 3)).reshape(1792, 512)
    vmem = functools.partial(pltpu.VMEM)
    nf, ns, wu = pl.pallas_call(
        kernel,
        out_shape=(
            jax.ShapeDtypeStruct((112, 128), F32),
            jax.ShapeDtypeStruct((112, 128), F32),
            jax.ShapeDtypeStruct((224, 1024), BF16),
        ),
        in_specs=[pl.BlockSpec(memory_space=pl.ANY)] * 5,
        out_specs=[pl.BlockSpec(memory_space=pltpu.VMEM)] * 3,
        scratch_shapes=[
            vmem((512, 1024), BF16),
            vmem((1024, 512), BF16),
            vmem((1792, 512), BF16),
            vmem((4, 1792, 128), F32),
            vmem((1792, 512), BF16),
            vmem((128, 128), F32),
            vmem((128, 128), F32),
            vmem((128, 128), F32),
            vmem((128, 128), F32),
            vmem((CH, 256, KC), BF16),
            vmem((CH, 256, KC), BF16),
            vmem((CH, 256, KC), F32),
            vmem((CH, 256, KC), BF16),
            vmem((CH, 256, KC), BF16),
            vmem((CH, 256, KC), BF16),
            vmem((CH, 256, KC), BF16),
            vmem((CH, 512, KC), BF16),
            vmem((CH, 4, 4, 112, KC), BF16),
            vmem((CH, 3, 4, 112, KC), BF16),
            vmem((CH, 4, 112, KC), BF16),
            vmem((CH, 3, 112, KC), BF16),
            vmem((CH, 128, KC), F32),
            vmem((CH, 4, 32, KC), BF16),
            vmem((CH, 3, 32, KC), BF16),
            vmem((CH, 8, 32, KC), BF16),
            vmem((CH, 232, KC), F32),
            vmem((224, 512), BF16),
            pltpu.SemaphoreType.DMA((5,)),
            pltpu.SemaphoreType.DMA((CH * SLOTS,)),
            pltpu.SemaphoreType.DMA((CH * SLOTS,)),
        ],
        compiler_params=pltpu.CompilerParams(
            collective_id=0, has_side_effects=True, vmem_limit_bytes=63 << 20
        ),
        name="galore_step",
    )(
        activations,
        projection_basis,
        cot,
        first_moment.reshape(112, 128),
        second_moment.reshape(112, 128),
    )
    return (
        nf.reshape(first_moment.shape),
        ns.reshape(second_moment.shape),
        jnp.transpose(wu).reshape(1024, 1, 224),
    )


def solution(mesh):
    in_specs = (
        P("dp", "tensor"),
        P("tensor", None),
        P(None, "tensor", None, "dp"),
        P("dp", "tensor", None, None),
        P("dp", "tensor", None, None),
    )
    out_specs = (
        P("dp", "tensor", None, None),
        P("dp", "tensor", None, None),
        P("tensor", "dp", None),
    )
    return jax.shard_map(
        per_device, mesh=mesh, in_specs=in_specs, out_specs=out_specs, check_vma=False
    )
```

```python
import functools

import jax
import jax.numpy as jnp
from jax import lax
from jax.experimental import pallas as pl
from jax.experimental.pallas import tpu as pltpu
from jax.sharding import PartitionSpec as P

STEP = 100
CH = 4
KC = 128
MESH = pl.DeviceIdType.MESH
F32, BF16 = jnp.float32, jnp.bfloat16

X0 = 0
E = X0 + CH
M = E + 2 * CH
T = M + 2 * CH
TC = T + 2 * CH
XY1 = TC + CH
XY2 = XY1 + 6 * CH
ZH = XY2 + 3 * CH
AG = ZH + 3 * CH // 2
SEMS = AG + 7 * CH // 2


def kernel(
    act_hbm, basis_hbm, cot_hbm, m1_hbm, m2_hbm,
    grad_ref, lhs_ref,
    act, basis, cot, cotf, cperm, m1, m2,
    x0s, x0r, acc, sb, er, mb, mr, proj,
    p2, ra, rb, rc, g, r2, hs, zs, r3, dirs, wide, grads,
    in_sem, send_sem, recv_sem,
):
    dp, tensor = lax.axis_index("dp"), lax.axis_index("tensor")
    zh, x, y = dp // 16, (dp // 4) % 4, dp % 4
    zl, c = tensor // 2, tensor % 2
    mid = jnp.logical_or(zl == 1, zl == 2)
    end = jnp.logical_not(mid)

    def at(zh=zh, x=x, y=y, zl=zl, c=c):
        return (zh * 16 + x * 4 + y, zl * 2 + c)

    def turn(v, i):
        return (v + i) % 4

    other_core = at(c=1 - c)
    pair = at(zl=zl + 1 - 2 * (zl % 2))
    middle = at(zl=3 - zl)
    xs = [at(x=turn(x, i)) for i in (1, 2, 3)]
    ys = [at(y=turn(y, i)) for i in (1, 2, 3)]
    zhs = [at(zh=turn(zh, i)) for i in (1, 2, 3)]
    steps = [(i, e) for i in range(4) for e in range(2)][1:]
    tensors = [at(zl=turn(zl, i), c=(c + e) % 2) for i, e in steps]

    barrier = pltpu.get_barrier_semaphore()
    for device in zhs + tensors + xs + ys:
        pl.semaphore_signal(barrier, inc=1, device_id=device, device_id_type=MESH)

    mine = pl.ds(pl.multiple_of(c * 256, 256), 256)
    theirs = pl.ds(pl.multiple_of((1 - c) * 256, 256), 256)

    loads = [
        pltpu.make_async_copy(basis_hbm, basis, in_sem.at[0]),
        pltpu.make_async_copy(act_hbm.at[theirs], act.at[theirs], in_sem.at[1]),
        pltpu.make_async_copy(act_hbm.at[mine], act.at[mine], in_sem.at[2]),
        pltpu.make_async_copy(cot_hbm, cot, in_sem.at[3]),
        pltpu.make_async_copy(m1_hbm, m1.at[pl.ds(0, 112)], in_sem.at[4]),
        pltpu.make_async_copy(m2_hbm, m2.at[pl.ds(0, 112)], in_sem.at[5]),
    ]
    for load in loads[:3]:
        load.start()

    def copy(i, src, dst, device):
        return pltpu.make_async_remote_copy(
            src, dst, send_sem.at[i], recv_sem.at[i], device_id=device, device_id_type=MESH
        )

    def half(h):
        return pl.ds(h * 128, 128)

    def proj_half(k, h):
        return proj.at[k, pl.ds(pl.multiple_of(c * 256 + h * 128, 128), 128)]

    def cp_x0(k):
        return copy(X0 + k, x0s.at[k], x0r.at[k], other_core)

    def cp_e(k, h):
        return copy(E + 2 * k + h, sb.at[k, half(h)], er.at[k, half(h)], pair)

    def cp_m(k, h):
        return copy(M + 2 * k + h, mb.at[k, half(h)], mr.at[k, half(h)], middle)

    def cp_t(k, h):
        return copy(T + 2 * k + h, proj_half(k, h), proj_half(k, h), pair)

    def cp_tc(k):
        return copy(TC + k, proj.at[k, mine], proj.at[k, mine], other_core)

    def tc_arrival(k):
        return copy(TC + k, proj.at[k, theirs], proj.at[k, theirs], other_core)

    def part(k, i, h):
        if k % 2 == 0:
            return p2.at[k, turn(x, i), pl.ds(2 * h, 2)]
        return p2.at[k, pl.ds(2 * h, 2), turn(y, i)]

    def cp_1(k, n):
        ring = xs if k % 2 == 0 else ys
        plus, minus = ring[0], ring[2]
        src, dst, device = (
            (part(k, 2, 0), ra.at[k, 0], plus),
            (part(k, 2, 1), ra.at[k, 1], minus),
            (part(k, 1, 1), rb.at[k, 0], plus),
            (part(k, 3, 0), rb.at[k, 1], minus),
            (part(k, 1, 0), rc.at[k, 0], plus),
            (part(k, 3, 1), rc.at[k, 1], minus),
        )[n]
        return copy(XY1 + 6 * k + n, src, dst, device)

    def cp_2(k, i):
        v, ring = (y, ys) if k % 2 == 0 else (x, xs)
        return copy(XY2 + 3 * k + i, g.at[k, turn(v, i + 1)], r2.at[k, i], ring[i])

    def cp_z(p, i):
        return copy(ZH + 3 * p + i, zs.at[p, turn(zh, i + 1)], r3.at[p, i], zhs[i])

    def cp_ag(p, n):
        return copy(AG + 7 * p + n, dirs.at[p, tensor], dirs.at[p, tensor], tensors[n])

    def ag_arrival(p, n):
        i, e = steps[n]
        slot = dirs.at[p, turn(zl, 4 - i) * 2 + (c + e) % 2]
        return copy(AG + 7 * p + n, slot, slot, tensors[n])

    loads[0].wait()
    loads[1].wait()
    for load in loads[3:]:
        load.start()
    out = jnp.dot(act[theirs, :], basis[...], preferred_element_type=F32)
    for k in range(CH):
        x0s[k] = out[:, k * KC : (k + 1) * KC].astype(BF16)
    pl.semaphore_wait(barrier, 16)
    for k in range(CH):
        cp_x0(k).start()
    loads[2].wait()
    out = jnp.dot(act[mine, :], basis[...], preferred_element_type=F32)
    for k in range(CH):
        acc[k] = out[:, k * KC : (k + 1) * KC]

    for k in range(CH):
        cp_x0(k).wait_recv()
        total = acc[k] + x0r[k].astype(F32)
        acc[k] = total

        @pl.when(end)
        def _():
            for h in range(2):
                sb[k, half(h)] = total[h * 128 : (h + 1) * 128].astype(BF16)
                cp_e(k, h).start()

    loads[3].wait()
    for n in range(4):
        cotf[n] = cot[:, n * 128 : (n + 1) * 128].astype(F32)
    for n in range(4):
        for b in range(16):
            cperm[pl.ds(b * 112, 112), n * 128 : (n + 1) * 128] = cotf[n, pl.ds(b, 112, stride=16), :].astype(BF16)
    for k in range(CH):
        hs[k, pl.ds(112, 16)] = jnp.zeros((16, KC), F32)
    m1[pl.ds(112, 16)] = jnp.zeros((16, KC), F32)
    m2[pl.ds(112, 16)] = jnp.zeros((16, KC), F32)

    def from_end(i):
        k, h = i // 2, i % 2
        cp_e(k, h).wait_recv()
        total = acc[k, half(h)] + er[k, half(h)].astype(F32)
        acc[k, half(h)] = total
        mb[k, half(h)] = total.astype(BF16)
        cp_m(k, h).start()

    def from_middle(i):
        k, h = i // 2, i % 2
        cp_m(k, h).wait_recv()
        rows = pl.ds(pl.multiple_of(c * 256 + h * 128, 128), 128)
        proj[k, rows] = (acc[k, half(h)] + mr[k, half(h)].astype(F32)).astype(BF16)
        cp_t(k, h).start()
        if h == 1:
            cp_tc(k).start()

    def to_end(i):
        k, h = i // 2, i % 2
        cp_t(k, h).wait_recv()
        if h == 1:
            cp_tc(k).start()

    def multiply(k):
        tc_arrival(k).wait_recv()
        out = jnp.dot(cperm[...], proj[k], preferred_element_type=F32)
        p2[k] = out.astype(BF16).reshape(4, 4, 112, KC)
        for n in range(4):
            cp_1(k, n).start()

    def pass_on(k):
        for h in range(2):
            cp_1(k, h).wait_recv()
            ref = part(k, 1 + 2 * h, h)
            ref[...] = (ref[...].astype(F32) + ra[k, h].astype(F32)).astype(BF16)
            cp_1(k, 4 + h).start()

    def first_sum(k):
        for h in range(2):
            cp_1(k, 3 - h).wait_recv()
            cp_1(k, 4 + h).wait_recv()
            total = part(k, 0, h)[...].astype(F32) + rb[k, 1 - h].astype(F32) + rc[k, h].astype(F32)
            g[k, pl.ds(2 * h, 2)] = total.astype(BF16)
        for i in range(3):
            cp_2(k, i).start()

    def second_sum(k):
        total = g[k, y if k % 2 == 0 else x].astype(F32)
        for i in range(3):
            cp_2(k, i).wait_recv()
            total = total + r2[k, i].astype(F32)
        hs[k, pl.ds(0, 112)] = total
        for z in range(4):
            zs[k // 2, z, k % 2] = hs[k, pl.ds(z, 32, stride=4), :].astype(BF16)
        if k % 2 == 1:
            for i in range(3):
                cp_z(k // 2, i).start()

    def adam(p):
        grad = zs[p, zh].astype(F32)
        for i in range(3):
            cp_z(p, i).wait_recv()
            grad = grad + r3[p, i].astype(F32)
        for j in range(2):
            rows = pl.ds(2 * p + j, 32, stride=4)
            low_rank = grad[j]
            grads[rows, :] = low_rank
            new_first = 0.9 * m1[rows, :] + 0.1 * low_rank
            new_second = 0.999 * m2[rows, :] + 0.001 * low_rank * low_rank
            direction = new_first / (1.0 - 0.9**STEP) / (jnp.sqrt(new_second / (1.0 - 0.999**STEP)) + 1e-08)
            dirs[p, tensor, j] = direction.astype(BF16)
        for n in range(7):
            cp_ag(p, n).start()

    def gathered(p):
        for n in range(7):
            ag_arrival(p, n).wait_recv()
        for j in range(2):
            k = 2 * p + j
            for t in range(8):
                wide[k, pl.ds(t * 28, 32)] = dirs[p, t, j].astype(F32)
            lhs_ref[:, k * KC : (k + 1) * KC] = wide[k, pl.ds(0, 224)].astype(BF16)

    @pl.when(mid)
    def _():
        for i in range(5):
            from_end(i)
        for i in range(3):
            from_middle(i)
            from_end(5 + i)
        from_middle(3)

    @pl.when(end)
    def _():
        for i in range(4):
            to_end(i)

    multiply(0)

    @pl.when(mid)
    def _():
        for i in (4, 5, 6):
            from_middle(i)

    @pl.when(end)
    def _():
        for i in (4, 5):
            to_end(i)

    multiply(1)

    @pl.when(mid)
    def _():
        from_middle(7)

    @pl.when(end)
    def _():
        for i in (6, 7):
            to_end(i)

    multiply(2)
    pass_on(0)
    multiply(3)
    for k in range(1, CH):
        pass_on(k)
    for k in range(CH):
        first_sum(k)
    for k in range(CH):
        second_sum(k)
    loads[4].wait()
    loads[5].wait()
    adam(0)
    adam(1)
    grad_ref[...] = grads[pl.ds(0, 112)]
    gathered(0)
    gathered(1)

    for k in range(CH):
        cp_x0(k).wait_send()
        cp_tc(k).wait_send()
        for n in range(6):
            cp_1(k, n).wait_send()
        for i in range(3):
            cp_2(k, i).wait_send()
    for p in range(CH // 2):
        for i in range(3):
            cp_z(p, i).wait_send()
        for n in range(7):
            cp_ag(p, n).wait_send()

    @pl.when(end)
    def _():
        for k in range(CH):
            for h in range(2):
                cp_e(k, h).wait_send()

    @pl.when(mid)
    def _():
        for k in range(CH):
            for h in range(2):
                cp_m(k, h).wait_send()
                cp_t(k, h).wait_send()


def per_device(activations, projection_basis, cotangent, first_moment, second_moment):
    cot = jnp.transpose(cotangent, (1, 2, 0, 3)).reshape(1792, 512)
    first, second = first_moment.reshape(112, 128), second_moment.reshape(112, 128)
    vmem = functools.partial(pltpu.VMEM)
    low_rank_grad, directions = pl.pallas_call(
        kernel,
        out_shape=(
            jax.ShapeDtypeStruct((112, 128), F32),
            jax.ShapeDtypeStruct((224, 512), BF16),
        ),
        in_specs=[pl.BlockSpec(memory_space=pltpu.HBM)] * 5,
        out_specs=[pl.BlockSpec(memory_space=pltpu.VMEM)] * 2,
        scratch_shapes=[
            vmem((512, 1024), BF16),
            vmem((1024, 512), BF16),
            vmem((1792, 512), BF16),
            vmem((4, 1792, 128), F32),
            vmem((1792, 512), BF16),
            vmem((128, 128), F32),
            vmem((128, 128), F32),
            vmem((CH, 256, KC), BF16),
            vmem((CH, 256, KC), BF16),
            vmem((CH, 256, KC), F32),
            vmem((CH, 256, KC), BF16),
            vmem((CH, 256, KC), BF16),
            vmem((CH, 256, KC), BF16),
            vmem((CH, 256, KC), BF16),
            vmem((CH, 512, KC), BF16),
            vmem((CH, 4, 4, 112, KC), BF16),
            vmem((CH, 2, 2, 112, KC), BF16),
            vmem((CH, 2, 2, 112, KC), BF16),
            vmem((CH, 2, 2, 112, KC), BF16),
            vmem((CH, 4, 112, KC), BF16),
            vmem((CH, 3, 112, KC), BF16),
            vmem((CH, 128, KC), F32),
            vmem((CH // 2, 4, 2, 32, KC), BF16),
            vmem((CH // 2, 3, 2, 32, KC), BF16),
            vmem((CH // 2, 8, 2, 32, KC), BF16),
            vmem((CH, 232, KC), F32),
            vmem((128, 128), F32),
            pltpu.SemaphoreType.DMA((6,)),
            pltpu.SemaphoreType.DMA((SEMS,)),
            pltpu.SemaphoreType.DMA((SEMS,)),
        ],
        compiler_params=pltpu.CompilerParams(
            collective_id=0, has_side_effects=True, vmem_limit_bytes=213 << 18
        ),
        name="galore_step",
    )(activations, projection_basis, cot, first, second)
    new_first = 0.9 * first + 0.1 * low_rank_grad
    new_second = 0.999 * second + 0.001 * low_rank_grad * low_rank_grad
    update = lax.dot_general(
        directions, projection_basis, (((1,), (1,)), ((), ())), preferred_element_type=F32
    ).astype(BF16)
    return (
        new_first.reshape(first_moment.shape),
        new_second.reshape(second_moment.shape),
        jnp.transpose(update).reshape(1024, 1, 224),
    )


def solution(mesh):
    in_specs = (
        P("dp", "tensor"),
        P("tensor", None),
        P(None, "tensor", None, "dp"),
        P("dp", "tensor", None, None),
        P("dp", "tensor", None, None),
    )
    out_specs = (
        P("dp", "tensor", None, None),
        P("dp", "tensor", None, None),
        P("tensor", "dp", None),
    )
    return jax.shard_map(
        per_device, mesh=mesh, in_specs=in_specs, out_specs=out_specs, check_vma=False
    )
```

```python
import functools

import jax
import jax.numpy as jnp
from jax import lax
from jax.experimental import pallas as pl
from jax.experimental.pallas import tpu as pltpu
from jax.sharding import PartitionSpec as P

STEP = 100
CH = 4
KC = 128
MESH = pl.DeviceIdType.MESH
F32, BF16 = jnp.float32, jnp.bfloat16

X0 = 0
E = X0 + CH
M = E + 2 * CH
T = M + 2 * CH
TC = T + 2 * CH
XY1 = TC + CH
XY2 = XY1 + 6 * CH
ZH = XY2 + 3 * CH
AG = ZH + 3 * CH // 2
SEMS = AG + 7 * CH // 2


def kernel(
    act_hbm, basis_hbm, cot_hbm, m1_hbm, m2_hbm,
    grad_ref, lhs_ref,
    act, basis, cot, cotf, cperm, m1, m2,
    x0s, x0r, acc, sb, er, mb, mr, proj,
    p2, ra, rb, rc, g, r2, hs, zs, r3, dirs, wide, grads,
    in_sem, send_sem, recv_sem,
):
    dp, tensor = lax.axis_index("dp"), lax.axis_index("tensor")
    zh, x, y = dp // 16, (dp // 4) % 4, dp % 4
    zl, c = tensor // 2, tensor % 2
    mid = jnp.logical_or(zl == 1, zl == 2)
    end = jnp.logical_not(mid)

    def at(zh=zh, x=x, y=y, zl=zl, c=c):
        return (zh * 16 + x * 4 + y, zl * 2 + c)

    def turn(v, i):
        return (v + i) % 4

    other_core = at(c=1 - c)
    pair = at(zl=zl + 1 - 2 * (zl % 2))
    middle = at(zl=3 - zl)
    xs = [at(x=turn(x, i)) for i in (1, 2, 3)]
    ys = [at(y=turn(y, i)) for i in (1, 2, 3)]
    zhs = [at(zh=turn(zh, i)) for i in (1, 2, 3)]
    steps = [(i, e) for i in range(4) for e in range(2)][1:]
    tensors = [at(zl=turn(zl, i), c=(c + e) % 2) for i, e in steps]

    barrier = pltpu.get_barrier_semaphore()
    for device in zhs + tensors + xs + ys:
        pl.semaphore_signal(barrier, inc=1, device_id=device, device_id_type=MESH)

    mine = pl.ds(pl.multiple_of(c * 256, 256), 256)
    theirs = pl.ds(pl.multiple_of((1 - c) * 256, 256), 256)

    loads = [
        pltpu.make_async_copy(basis_hbm, basis, in_sem.at[0]),
        pltpu.make_async_copy(act_hbm.at[theirs], act.at[theirs], in_sem.at[1]),
        pltpu.make_async_copy(act_hbm.at[mine], act.at[mine], in_sem.at[2]),
        pltpu.make_async_copy(cot_hbm, cot, in_sem.at[3]),
        pltpu.make_async_copy(m1_hbm, m1.at[pl.ds(0, 112)], in_sem.at[4]),
        pltpu.make_async_copy(m2_hbm, m2.at[pl.ds(0, 112)], in_sem.at[5]),
    ]
    for load in loads[:3]:
        load.start()

    def copy(i, src, dst, device):
        return pltpu.make_async_remote_copy(
            src, dst, send_sem.at[i], recv_sem.at[i], device_id=device, device_id_type=MESH
        )

    def half(h):
        return pl.ds(h * 128, 128)

    def proj_half(k, h):
        return proj.at[k, pl.ds(pl.multiple_of(c * 256 + h * 128, 128), 128)]

    def cp_x0(k):
        return copy(X0 + k, x0s.at[k], x0r.at[k], other_core)

    def cp_e(k, h):
        return copy(E + 2 * k + h, sb.at[k, half(h)], er.at[k, half(h)], pair)

    def cp_m(k, h):
        return copy(M + 2 * k + h, mb.at[k, half(h)], mr.at[k, half(h)], middle)

    def cp_t(k, h):
        return copy(T + 2 * k + h, proj_half(k, h), proj_half(k, h), pair)

    def cp_tc(k):
        return copy(TC + k, proj.at[k, mine], proj.at[k, mine], other_core)

    def tc_arrival(k):
        return copy(TC + k, proj.at[k, theirs], proj.at[k, theirs], other_core)

    def part(k, i, h):
        if k % 2 == 0:
            return p2.at[k, turn(x, i), pl.ds(2 * h, 2)]
        return p2.at[k, pl.ds(2 * h, 2), turn(y, i)]

    def cp_1(k, n):
        ring = xs if k % 2 == 0 else ys
        plus, minus = ring[0], ring[2]
        src, dst, device = (
            (part(k, 2, 0), ra.at[k, 0], plus),
            (part(k, 2, 1), ra.at[k, 1], minus),
            (part(k, 1, 1), rb.at[k, 0], plus),
            (part(k, 3, 0), rb.at[k, 1], minus),
            (part(k, 1, 0), rc.at[k, 0], plus),
            (part(k, 3, 1), rc.at[k, 1], minus),
        )[n]
        return copy(XY1 + 6 * k + n, src, dst, device)

    def cp_2(k, i):
        v, ring = (y, ys) if k % 2 == 0 else (x, xs)
        return copy(XY2 + 3 * k + i, g.at[k, turn(v, i + 1)], r2.at[k, i], ring[i])

    def cp_z(p, i):
        return copy(ZH + 3 * p + i, zs.at[p, turn(zh, i + 1)], r3.at[p, i], zhs[i])

    def cp_ag(p, n):
        return copy(AG + 7 * p + n, dirs.at[p, tensor], dirs.at[p, tensor], tensors[n])

    def ag_arrival(p, n):
        i, e = steps[n]
        slot = dirs.at[p, turn(zl, 4 - i) * 2 + (c + e) % 2]
        return copy(AG + 7 * p + n, slot, slot, tensors[n])

    loads[0].wait()
    loads[1].wait()
    for load in loads[3:]:
        load.start()
    out = jnp.dot(act[theirs, :], basis[...], preferred_element_type=F32)
    for k in range(CH):
        x0s[k] = out[:, k * KC : (k + 1) * KC].astype(BF16)
    pl.semaphore_wait(barrier, 16)
    for k in range(CH):
        cp_x0(k).start()
    loads[2].wait()
    out = jnp.dot(act[mine, :], basis[...], preferred_element_type=F32)
    for k in range(CH):
        acc[k] = out[:, k * KC : (k + 1) * KC]

    for k in range(CH):
        cp_x0(k).wait_recv()
        total = acc[k] + x0r[k].astype(F32)
        acc[k] = total

        @pl.when(end)
        def _():
            for h in range(2):
                sb[k, half(h)] = total[h * 128 : (h + 1) * 128].astype(BF16)
                cp_e(k, h).start()

    loads[3].wait()
    for n in range(4):
        cotf[n] = cot[:, n * 128 : (n + 1) * 128].astype(F32)
    for n in range(4):
        for b in range(16):
            cperm[pl.ds(b * 112, 112), n * 128 : (n + 1) * 128] = cotf[n, pl.ds(b, 112, stride=16), :].astype(BF16)
    for k in range(CH):
        hs[k, pl.ds(112, 16)] = jnp.zeros((16, KC), F32)
    m1[pl.ds(112, 16)] = jnp.zeros((16, KC), F32)
    m2[pl.ds(112, 16)] = jnp.zeros((16, KC), F32)

    def from_end(i):
        k, h = i // 2, i % 2
        cp_e(k, h).wait_recv()
        total = acc[k, half(h)] + er[k, half(h)].astype(F32)
        acc[k, half(h)] = total
        mb[k, half(h)] = total.astype(BF16)
        cp_m(k, h).start()

    def from_middle(i):
        k, h = i // 2, i % 2
        cp_m(k, h).wait_recv()
        rows = pl.ds(pl.multiple_of(c * 256 + h * 128, 128), 128)
        proj[k, rows] = (acc[k, half(h)] + mr[k, half(h)].astype(F32)).astype(BF16)
        cp_t(k, h).start()
        if h == 1:
            cp_tc(k).start()

    def to_end(i):
        k, h = i // 2, i % 2
        cp_t(k, h).wait_recv()
        if h == 1:
            cp_tc(k).start()

    def multiply(k):
        tc_arrival(k).wait_recv()
        out = jnp.dot(cperm[...], proj[k], preferred_element_type=F32)
        p2[k] = out.astype(BF16).reshape(4, 4, 112, KC)
        for n in range(4):
            cp_1(k, n).start()

    def pass_on(k):
        for h in range(2):
            cp_1(k, h).wait_recv()
            ref = part(k, 1 + 2 * h, h)
            ref[...] = (ref[...].astype(F32) + ra[k, h].astype(F32)).astype(BF16)
            cp_1(k, 4 + h).start()

    def first_sum(k):
        for h in range(2):
            cp_1(k, 3 - h).wait_recv()
            cp_1(k, 4 + h).wait_recv()
            total = part(k, 0, h)[...].astype(F32) + rb[k, 1 - h].astype(F32) + rc[k, h].astype(F32)
            g[k, pl.ds(2 * h, 2)] = total.astype(BF16)
        for i in range(3):
            cp_2(k, i).start()

    def second_sum(k):
        total = g[k, y if k % 2 == 0 else x].astype(F32)
        for i in range(3):
            cp_2(k, i).wait_recv()
            total = total + r2[k, i].astype(F32)
        hs[k, pl.ds(0, 112)] = total
        for z in range(4):
            zs[k // 2, z, k % 2] = hs[k, pl.ds(z, 32, stride=4), :].astype(BF16)
        if k % 2 == 1:
            for i in range(3):
                cp_z(k // 2, i).start()

    def adam(p):
        grad = zs[p, zh].astype(F32)
        for i in range(3):
            cp_z(p, i).wait_recv()
            grad = grad + r3[p, i].astype(F32)
        for j in range(2):
            rows = pl.ds(2 * p + j, 32, stride=4)
            low_rank = grad[j]
            grads[rows, :] = low_rank
            new_first = 0.9 * m1[rows, :] + 0.1 * low_rank
            new_second = 0.999 * m2[rows, :] + 0.001 * low_rank * low_rank
            direction = new_first / (1.0 - 0.9**STEP) / (jnp.sqrt(new_second / (1.0 - 0.999**STEP)) + 1e-08)
            dirs[p, tensor, j] = direction.astype(BF16)
        for n in range(7):
            cp_ag(p, n).start()

    def gathered(p):
        for n in range(7):
            ag_arrival(p, n).wait_recv()
        for j in range(2):
            k = 2 * p + j
            for t in range(8):
                wide[k, pl.ds(t * 28, 32)] = dirs[p, t, j].astype(F32)
            lhs_ref[:, k * KC : (k + 1) * KC] = wide[k, pl.ds(0, 224)].astype(BF16)

    @pl.when(mid)
    def _():
        for i in range(5):
            from_end(i)
        for i in range(3):
            from_middle(i)
            from_end(5 + i)
        from_middle(3)

    @pl.when(end)
    def _():
        for i in range(4):
            to_end(i)

    multiply(0)

    @pl.when(mid)
    def _():
        for i in (4, 5, 6):
            from_middle(i)

    @pl.when(end)
    def _():
        for i in (4, 5):
            to_end(i)

    multiply(1)

    @pl.when(mid)
    def _():
        from_middle(7)

    @pl.when(end)
    def _():
        for i in (6, 7):
            to_end(i)

    multiply(2)
    pass_on(0)
    multiply(3)
    for k in range(1, CH):
        pass_on(k)
    for k in range(CH):
        first_sum(k)
    for k in range(CH):
        second_sum(k)
    loads[4].wait()
    loads[5].wait()
    adam(0)
    adam(1)
    grad_ref[...] = grads[pl.ds(0, 112)]
    gathered(0)
    gathered(1)

    for k in range(CH):
        cp_x0(k).wait_send()
        cp_tc(k).wait_send()
        for n in range(6):
            cp_1(k, n).wait_send()
        for i in range(3):
            cp_2(k, i).wait_send()
    for p in range(CH // 2):
        for i in range(3):
            cp_z(p, i).wait_send()
        for n in range(7):
            cp_ag(p, n).wait_send()

    @pl.when(end)
    def _():
        for k in range(CH):
            for h in range(2):
                cp_e(k, h).wait_send()

    @pl.when(mid)
    def _():
        for k in range(CH):
            for h in range(2):
                cp_m(k, h).wait_send()
                cp_t(k, h).wait_send()


def finish(grad_ref, lhs_ref, basis_ref, m1_ref, m2_ref, nf_hbm, ns_hbm, wu_hbm, nf, ns, wu, sem):
    outs = [
        pltpu.make_async_copy(nf, nf_hbm, sem.at[0]),
        pltpu.make_async_copy(ns, ns_hbm, sem.at[1]),
    ] + [
        pltpu.make_async_copy(wu.at[:, pl.ds(n * 512, 512)], wu_hbm.at[:, pl.ds(n * 512, 512)], sem.at[2 + n])
        for n in range(2)
    ]
    low_rank = grad_ref[...]
    nf[...] = 0.9 * m1_ref[...] + 0.1 * low_rank
    ns[...] = 0.999 * m2_ref[...] + 0.001 * low_rank * low_rank
    outs[0].start()
    outs[1].start()
    for n in range(2):
        wu[:, n * 512 : (n + 1) * 512] = lax.dot_general(
            lhs_ref[...], basis_ref[n * 512 : (n + 1) * 512, :], (((1,), (1,)), ((), ())),
            preferred_element_type=F32,
        ).astype(BF16)
        outs[2 + n].start()
    for out in outs:
        out.wait()


def per_device(activations, projection_basis, cotangent, first_moment, second_moment):
    cot = jnp.transpose(cotangent, (1, 2, 0, 3)).reshape(1792, 512)
    first, second = first_moment.reshape(112, 128), second_moment.reshape(112, 128)
    vmem = functools.partial(pltpu.VMEM)
    low_rank_grad, directions = pl.pallas_call(
        kernel,
        out_shape=(
            jax.ShapeDtypeStruct((112, 128), F32),
            jax.ShapeDtypeStruct((224, 512), BF16),
        ),
        in_specs=[pl.BlockSpec(memory_space=pltpu.HBM)] * 5,
        out_specs=[pl.BlockSpec(memory_space=pltpu.VMEM)] * 2,
        scratch_shapes=[
            vmem((512, 1024), BF16),
            vmem((1024, 512), BF16),
            vmem((1792, 512), BF16),
            vmem((4, 1792, 128), F32),
            vmem((1792, 512), BF16),
            vmem((128, 128), F32),
            vmem((128, 128), F32),
            vmem((CH, 256, KC), BF16),
            vmem((CH, 256, KC), BF16),
            vmem((CH, 256, KC), F32),
            vmem((CH, 256, KC), BF16),
            vmem((CH, 256, KC), BF16),
            vmem((CH, 256, KC), BF16),
            vmem((CH, 256, KC), BF16),
            vmem((CH, 512, KC), BF16),
            vmem((CH, 4, 4, 112, KC), BF16),
            vmem((CH, 2, 2, 112, KC), BF16),
            vmem((CH, 2, 2, 112, KC), BF16),
            vmem((CH, 2, 2, 112, KC), BF16),
            vmem((CH, 4, 112, KC), BF16),
            vmem((CH, 3, 112, KC), BF16),
            vmem((CH, 128, KC), F32),
            vmem((CH // 2, 4, 2, 32, KC), BF16),
            vmem((CH // 2, 3, 2, 32, KC), BF16),
            vmem((CH // 2, 8, 2, 32, KC), BF16),
            vmem((CH, 232, KC), F32),
            vmem((128, 128), F32),
            pltpu.SemaphoreType.DMA((6,)),
            pltpu.SemaphoreType.DMA((SEMS,)),
            pltpu.SemaphoreType.DMA((SEMS,)),
        ],
        compiler_params=pltpu.CompilerParams(
            collective_id=0, has_side_effects=True, vmem_limit_bytes=213 << 18
        ),
        name="galore_step",
    )(activations, projection_basis, cot, first, second)
    new_first, new_second, update = pl.pallas_call(
        finish,
        out_shape=(
            jax.ShapeDtypeStruct((112, 128), F32),
            jax.ShapeDtypeStruct((112, 128), F32),
            jax.ShapeDtypeStruct((224, 1024), BF16),
        ),
        in_specs=[pl.BlockSpec(memory_space=pltpu.VMEM)] * 5,
        out_specs=[pl.BlockSpec(memory_space=pltpu.HBM)] * 3,
        scratch_shapes=[
            vmem((112, 128), F32),
            vmem((112, 128), F32),
            vmem((224, 1024), BF16),
            pltpu.SemaphoreType.DMA((4,)),
        ],
        compiler_params=pltpu.CompilerParams(vmem_limit_bytes=16 << 20),
        name="finish_step",
    )(low_rank_grad, directions, projection_basis, first, second)
    return (
        new_first.reshape(first_moment.shape),
        new_second.reshape(second_moment.shape),
        jnp.transpose(update).reshape(1024, 1, 224),
    )


def solution(mesh):
    in_specs = (
        P("dp", "tensor"),
        P("tensor", None),
        P(None, "tensor", None, "dp"),
        P("dp", "tensor", None, None),
        P("dp", "tensor", None, None),
    )
    out_specs = (
        P("dp", "tensor", None, None),
        P("dp", "tensor", None, None),
        P("tensor", "dp", None),
    )
    return jax.shard_map(
        per_device, mesh=mesh, in_specs=in_specs, out_specs=out_specs, check_vma=False
    )
```
